32 devices in a mesh: row: 4 (over x, core), col: 4 (over z), seq: 2 (over y).
Axes of the slice: x: 2, y: 2, z: 4, core: 2. Of those that a mesh axis runs over, the one named last changes fastest.
Arguments:
- ffn_input: bfloat16 [1024, 6144], P('seq', 'row'), may hold values from -6 to 6
- attn_mix: bfloat16 [1024, 6144], P('seq', 'col'), may hold values from -6 to 6
- out_grad: bfloat16 [1024, 6144], P('seq', 'row'), may hold values from -6 to 6
- w_gate: bfloat16 [6144, 16384], P('row', 'col'), may hold values from -0.078125 to 0.078125
- w_up: bfloat16 [6144, 16384], P('row', 'col'), may hold values from -0.078125 to 0.078125
- w_down: bfloat16 [6144, 16384], P('row', 'col'), may hold values from -0.046875 to 0.046875
- w_out: bfloat16 [6144, 6144], P('row', 'col'), may hold values from -0.078125 to 0.078125
Outputs:
- resid_grad: bfloat16 [1024, 6144], P('seq', 'row')
- attn_grad: bfloat16 [1024, 6144], P('seq', 'col')
- gate_wgrad: float32 [6144, 16384], P('row', ('col', 'seq'))
- up_wgrad: float32 [6144, 16384], P('row', ('col', 'seq'))
- down_wgrad: float32 [6144, 16384], P('row', ('col', 'seq'))
- out_wgrad: float32 [6144, 6144], P('row', ('col', 'seq'))
The draws below stay inside these ranges and needn't reach their ends.
All inputs are finite; a program needn't handle non-finite values.
Results may differ from the reference program's by a relative error of at most 0.01.
Values may be sent and summed in bfloat16 or wider, within the bound.
A program may use at most 320 MiB of HBM per device.

```python
import jax
import jax.numpy as jnp

D = 6144
FF = 16384
TOKENS = 1024


def level_of(rng, shape, pieces, low, largest):
    def one(dim, parts):
        heights = jax.random.uniform(jax.random.fold_in(jax.random.fold_in(rng, 6), dim), (parts,), jnp.float32, low / len(pieces), largest / len(pieces))
        return jnp.repeat(jnp.exp(heights), shape[dim] // parts).reshape((-1,) + (1,) * (len(shape) - dim - 1))

    loudness = one(*pieces[0])
    for cut in pieces[1:]:
        loudness = loudness * one(*cut)
    return loudness


def bell_draw(key, shape, deviation, reach, split=(), kind=jnp.bfloat16):
    drawn = deviation * jax.random.normal(key, shape, jnp.float32)
    if split:
        drawn = drawn * level_of(key, shape, split, -0.22, 0.18)
    return jnp.clip(drawn, -reach, reach).astype(kind)


def setup_inputs(seed: int = 0) -> dict:
    seeds = jax.random.split(jax.random.key(seed), 8)
    ffn_input = bell_draw(seeds[0], (TOKENS, D), 1.0, 6.0, ((0, 2), (1, 4)))
    attn_mix = bell_draw(seeds[1], (TOKENS, D), 1.0, 6.0, ((0, 2), (1, 4)))
    out_grad = bell_draw(seeds[2], (TOKENS, D), 1.0, 6.0, ((0, 2), (1, 4)))
    w_gate = bell_draw(seeds[3], (D, FF), D ** -0.5, 0.078125, ((0, 4), (1, 4)))
    w_up = bell_draw(seeds[4], (D, FF), D ** -0.5, 0.078125, ((0, 4), (1, 4)))
    w_down = bell_draw(seeds[5], (D, FF), FF ** -0.5, 0.046875, ((0, 4), (1, 4)))
    w_out = bell_draw(seeds[6], (D, D), D ** -0.5, 0.078125, ((0, 4), (1, 4)))
    return dict(ffn_input=ffn_input, attn_mix=attn_mix, out_grad=out_grad, w_gate=w_gate, w_up=w_up, w_down=w_down, w_out=w_out)


def swiglu_grads(gate_pre, up_pre, hidden_grad):
    sigmoid_gate = jax.nn.sigmoid(gate_pre)
    activated = gate_pre * sigmoid_gate
    hidden = (activated * up_pre).astype(jnp.bfloat16)
    up_grad = (hidden_grad * activated).astype(jnp.bfloat16)
    slope = sigmoid_gate * (1.0 + gate_pre * (1.0 - sigmoid_gate))
    gate_grad = (hidden_grad * up_pre * slope).astype(jnp.bfloat16)
    return gate_grad, up_grad, hidden


def reference(ffn_input, attn_mix, out_grad, w_gate, w_up, w_down, w_out):
    gate_pre = jnp.dot(ffn_input, w_gate, preferred_element_type=jnp.float32)
    up_pre = jnp.dot(ffn_input, w_up, preferred_element_type=jnp.float32)
    hidden_grad = jnp.dot(out_grad, w_down, preferred_element_type=jnp.float32)
    gate_grad, up_grad, hidden = swiglu_grads(gate_pre, up_pre, hidden_grad)
    back_sum = jnp.dot(gate_grad, w_gate.T, preferred_element_type=jnp.float32) + jnp.dot(up_grad, w_up.T, preferred_element_type=jnp.float32)
    resid_grad = (out_grad.astype(jnp.float32) + back_sum).astype(jnp.bfloat16)
    attn_grad = jnp.dot(resid_grad, w_out, preferred_element_type=jnp.float32).astype(jnp.bfloat16)
    norm_factor = TOKENS ** -0.5
    gate_wgrad = jnp.dot(ffn_input.T, gate_grad, preferred_element_type=jnp.float32) * norm_factor
    up_wgrad = jnp.dot(ffn_input.T, up_grad, preferred_element_type=jnp.float32) * norm_factor
    down_wgrad = jnp.dot(out_grad.T, hidden, preferred_element_type=jnp.float32) * norm_factor
    out_wgrad = jnp.dot(resid_grad.T, attn_mix, preferred_element_type=jnp.float32) * norm_factor
    return resid_grad, attn_grad, gate_wgrad, up_wgrad, down_wgrad, out_wgrad
```

```python
import jax
import jax.numpy as jnp
from jax import lax
from jax.sharding import PartitionSpec as P

BF16 = jnp.bfloat16
F32 = jnp.float32


def swiglu_grads(gate_pre, up_pre, hidden_grad):
    sigmoid_gate = jax.nn.sigmoid(gate_pre)
    activated = gate_pre * sigmoid_gate
    hidden = (activated * up_pre).astype(BF16)
    up_grad = (hidden_grad * activated).astype(BF16)
    slope = sigmoid_gate * (1.0 + gate_pre * (1.0 - sigmoid_gate))
    gate_grad = (hidden_grad * up_pre * slope).astype(BF16)
    return (gate_grad, up_grad, hidden)


def dot(first, second):
    return jnp.dot(first, second, preferred_element_type=F32)


def contract_rows(first, second):
    return lax.dot_general(
        first, second, (((0,), (0,)), ((), ())), preferred_element_type=F32
    )


def contract_cols(first, second):
    return lax.dot_general(
        first, second, (((1,), (1,)), ((), ())), preferred_element_type=F32
    )


def swap(value, axis, bit):
    size = lax.axis_size(axis)
    return lax.ppermute(value, axis, [(i, i ^ bit) for i in range(size)])


def chip_sum(part):
    size = lax.axis_size("row")
    bit = 2
    while bit < size:
        mine = part.astype(BF16)
        part = mine.astype(F32) + swap(mine, "row", bit).astype(F32)
        bit *= 2
    return part


def chip_sum_wide(part):
    size = lax.axis_size("row")
    bit = 2
    while bit < size:
        part = part + swap(part.astype(BF16), "row", bit).astype(F32)
        bit *= 2
    return part


def in_order(core, mine, theirs, axis):
    return jnp.where(
        core == 0,
        jnp.concatenate([mine, theirs], axis),
        jnp.concatenate([theirs, mine], axis),
    )


def col_scatter(part):
    place = lax.axis_index("col")
    bit = 1
    while bit < lax.axis_size("col"):
        half = part.shape[0] // 2
        high = (place // bit) % 2
        sent = lax.dynamic_slice_in_dim(part, (1 - high) * half, half, 0)
        kept = lax.dynamic_slice_in_dim(part, high * half, half, 0)
        part = kept + swap(sent.astype(BF16), "col", bit).astype(F32)
        bit *= 2
    return part


def col_share(value):
    place = lax.axis_index("col")
    bit = 1
    while bit < lax.axis_size("col"):
        half = value.shape[0] // 2
        high = (place // bit) % 2
        value = lax.dynamic_slice_in_dim(value, high * half, half, 0)
        bit *= 2
    return value


def col_gather(value):
    place = lax.axis_index("col")
    bit = lax.axis_size("col") // 2
    while bit >= 1:
        high = (place // bit) % 2
        value = in_order(high, value, swap(value, "col", bit), 0)
        bit //= 2
    return value


def per_device(ffn_input, attn_mix, out_grad, w_gate, w_up, w_down, w_out):
    core = lax.axis_index("row") % 2
    seq = lax.axis_index("seq")
    tokens, width = ffn_input.shape
    hidden_half = w_gate.shape[1] // 2
    quarter = hidden_half // 2
    head_half = attn_mix.shape[1] // 2
    step = tokens // 2
    norm_factor = (tokens * lax.axis_size("seq")) ** (-0.5)

    own_chunks = [
        (ffn_input[i : i + step], out_grad[i : i + step]) for i in (0, step)
    ]
    other_chunks = [(swap(f, "seq", 1), swap(g, "seq", 1)) for f, g in own_chunks]
    mix_sent = lax.dynamic_slice_in_dim(attn_mix, (1 - seq) * head_half, head_half, 1)
    mix_kept = lax.dynamic_slice_in_dim(attn_mix, seq * head_half, head_half, 1)
    mix_other = swap(mix_sent, "seq", 1)

    def columns(weight, which):
        start = seq * hidden_half + which * quarter
        return lax.dynamic_slice_in_dim(weight, start, quarter, 1)

    mine = [columns(w, core) for w in (w_gate, w_up, w_down)]
    theirs = [columns(w, 1 - core) for w in (w_gate, w_up, w_down)]

    def forward(chunk):
        f, g = chunk
        sums = []
        for x, w_mine, w_theirs in zip((f, f, g), mine, theirs):
            sent = dot(x, w_theirs).astype(BF16)
            part = dot(x, w_mine) + swap(sent, "row", 1).astype(F32)
            sums.append(chip_sum_wide(part))
        own = swiglu_grads(*sums)
        sibling = [swap(v, "row", 1) for v in own]
        back = (
            contract_cols(own[0], mine[0])
            + contract_cols(own[1], mine[1])
            + contract_cols(sibling[0], theirs[0])
            + contract_cols(sibling[1], theirs[1])
        )
        whole = [in_order(core, a, b, 1) for a, b in zip(own, sibling)]
        return back, whole

    w_out_mine = lax.dynamic_slice_in_dim(w_out, core * head_half, head_half, 1)
    w_out_theirs = lax.dynamic_slice_in_dim(w_out, (1 - core) * head_half, head_half, 1)

    def finish(back, received, grad_chunk):
        total = col_scatter(back + received.astype(F32))
        share = (col_share(grad_chunk).astype(F32) + total).astype(BF16)
        resid = col_gather(share)
        resid_other = swap(resid, "seq", 1)
        sent = dot(resid, w_out_theirs).astype(BF16)
        part = dot(resid, w_out_mine) + swap(sent, "row", 1).astype(F32)
        attn = chip_sum(part).astype(BF16)
        attn = in_order(core, attn, swap(attn, "row", 1), 1)
        return resid, resid_other, attn

    back_own0, whole_own0 = forward(own_chunks[0])
    back_other0, whole_other0 = forward(other_chunks[0])
    received0 = swap(back_other0.astype(BF16), "seq", 1)
    back_other1, whole_other1 = forward(other_chunks[1])
    received1 = swap(back_other1.astype(BF16), "seq", 1)
    resid0, resid_other0, attn0 = finish(back_own0, received0, own_chunks[0][1])
    back_own1, whole_own1 = forward(own_chunks[1])
    resid1, resid_other1, attn1 = finish(back_own1, received1, own_chunks[1][1])

    gate_grad, up_grad, hidden = (
        jnp.concatenate(v, 0)
        for v in zip(whole_own0, whole_own1, whole_other0, whole_other1)
    )
    ffn_all = jnp.concatenate([ffn_input, other_chunks[0][0], other_chunks[1][0]], 0)
    grad_all = jnp.concatenate([out_grad, other_chunks[0][1], other_chunks[1][1]], 0)
    gate_wgrad = contract_rows(ffn_all, gate_grad) * norm_factor
    up_wgrad = contract_rows(ffn_all, up_grad) * norm_factor
    down_wgrad = contract_rows(grad_all, hidden) * norm_factor

    resid_grad = jnp.concatenate([resid0, resid1], 0)
    attn_grad = jnp.concatenate([attn0, attn1], 0)
    resid_all = jnp.concatenate([resid_grad, resid_other0, resid_other1], 0)
    mix_all = jnp.concatenate([mix_kept, mix_other], 0)
    out_wgrad = contract_rows(resid_all, mix_all) * norm_factor
    return (resid_grad, attn_grad, gate_wgrad, up_wgrad, down_wgrad, out_wgrad)


def solution(mesh):
    return jax.shard_map(
        per_device,
        mesh=mesh,
        in_specs=(
            P("seq", "row"),
            P("seq", "col"),
            P("seq", "row"),
            P("row", "col"),
            P("row", "col"),
            P("row", "col"),
            P("row", "col"),
        ),
        out_specs=(
            P("seq", "row"),
            P("seq", "col"),
            P("row", ("col", "seq")),
            P("row", ("col", "seq")),
            P("row", ("col", "seq")),
            P("row", ("col", "seq")),
        ),
        check_vma=False,
    )
```

```python
import jax
import jax.numpy as jnp
from jax import lax
from jax.sharding import PartitionSpec as P

BF16 = jnp.bfloat16
F32 = jnp.float32


def swiglu_grads(gate_pre, up_pre, hidden_grad):
    sigmoid_gate = jax.nn.sigmoid(gate_pre)
    activated = gate_pre * sigmoid_gate
    hidden = (activated * up_pre).astype(BF16)
    up_grad = (hidden_grad * activated).astype(BF16)
    slope = sigmoid_gate * (1.0 + gate_pre * (1.0 - sigmoid_gate))
    gate_grad = (hidden_grad * up_pre * slope).astype(BF16)
    return (gate_grad, up_grad, hidden)


def dot(first, second):
    return jnp.dot(first, second, preferred_element_type=F32)


def contract_rows(first, second):
    return lax.dot_general(
        first, second, (((0,), (0,)), ((), ())), preferred_element_type=F32
    )


def contract_cols(first, second):
    return lax.dot_general(
        first, second, (((1,), (1,)), ((), ())), preferred_element_type=F32
    )


def swap(value, axis, bit):
    size = lax.axis_size(axis)
    return lax.ppermute(value, axis, [(i, i ^ bit) for i in range(size)])


def after(value, earlier):
    return lax.optimization_barrier((value, earlier))[0]


def chip_sum(part):
    size = lax.axis_size("row")
    bit = 2
    while bit < size:
        mine = part.astype(BF16)
        part = mine.astype(F32) + swap(mine, "row", bit).astype(F32)
        bit *= 2
    return part


def chip_sum_wide(part):
    size = lax.axis_size("row")
    bit = 2
    received = part
    while bit < size:
        received = swap(part.astype(BF16), "row", bit)
        part = part + received.astype(F32)
        bit *= 2
    return part, received


def in_order(core, mine, theirs, axis):
    return jnp.where(
        core == 0,
        jnp.concatenate([mine, theirs], axis),
        jnp.concatenate([theirs, mine], axis),
    )


def col_scatter(part):
    place = lax.axis_index("col")
    bit = 1
    while bit < lax.axis_size("col"):
        half = part.shape[0] // 2
        high = (place // bit) % 2
        sent = lax.dynamic_slice_in_dim(part, (1 - high) * half, half, 0)
        kept = lax.dynamic_slice_in_dim(part, high * half, half, 0)
        part = kept + swap(sent.astype(BF16), "col", bit).astype(F32)
        bit *= 2
    return part


def col_share(value):
    place = lax.axis_index("col")
    bit = 1
    while bit < lax.axis_size("col"):
        half = value.shape[0] // 2
        high = (place // bit) % 2
        value = lax.dynamic_slice_in_dim(value, high * half, half, 0)
        bit *= 2
    return value


def col_gather(value):
    place = lax.axis_index("col")
    bit = lax.axis_size("col") // 2
    while bit >= 1:
        high = (place // bit) % 2
        value = in_order(high, value, swap(value, "col", bit), 0)
        bit //= 2
    return value


def per_device(ffn_input, attn_mix, out_grad, w_gate, w_up, w_down, w_out):
    core = lax.axis_index("row") % 2
    seq = lax.axis_index("seq")
    tokens, width = ffn_input.shape
    hidden_half = w_gate.shape[1] // 2
    quarter = hidden_half // 2
    head_half = attn_mix.shape[1] // 2
    step = tokens // 2
    norm_factor = (tokens * lax.axis_size("seq")) ** (-0.5)

    own_a = (ffn_input[:step], out_grad[:step])
    own_b = (ffn_input[step:], out_grad[step:])
    ffn_other = swap(ffn_input, "seq", 1)
    grad_other = swap(after(out_grad, ffn_other), "seq", 1)
    mix_sent = lax.dynamic_slice_in_dim(attn_mix, (1 - seq) * head_half, head_half, 1)
    mix_kept = lax.dynamic_slice_in_dim(attn_mix, seq * head_half, head_half, 1)
    mix_other = swap(after(mix_sent, grad_other), "seq", 1)

    def columns(weight, which):
        start = seq * hidden_half + which * quarter
        return lax.dynamic_slice_in_dim(weight, start, quarter, 1)

    mine = [columns(w, core) for w in (w_gate, w_up, w_down)]
    theirs = [columns(w, 1 - core) for w in (w_gate, w_up, w_down)]

    parts, arrived = [], []

    def forward(chunk):
        f, g = chunk
        sums = []
        for x, w_mine, w_theirs in zip((f, f, g), mine, theirs):
            if parts:
                x = after(x, parts[-1])
            if len(arrived) >= 3:
                x = after(x, arrived[-3])
            sent = dot(x, w_theirs).astype(BF16)
            parts.append(dot(x, w_mine) + swap(sent, "row", 1).astype(F32))
            total, received = chip_sum_wide(parts[-1])
            sums.append(total)
            arrived.append(received)
        return sums

    def backward(sums):
        own = swiglu_grads(*sums)
        sibling = [swap(v, "row", 1) for v in own]
        back = (
            contract_cols(own[0], mine[0])
            + contract_cols(own[1], mine[1])
            + contract_cols(sibling[0], theirs[0])
            + contract_cols(sibling[1], theirs[1])
        )
        whole = [in_order(core, a, b, 1) for a, b in zip(own, sibling)]
        return back, whole

    w_out_mine = lax.dynamic_slice_in_dim(w_out, core * head_half, head_half, 1)
    w_out_theirs = lax.dynamic_slice_in_dim(w_out, (1 - core) * head_half, head_half, 1)

    def finish(back, received, grad_chunk):
        total = col_scatter(back + received.astype(F32))
        share = (col_share(grad_chunk).astype(F32) + total).astype(BF16)
        resid = col_gather(share)
        resid_other = swap(resid, "seq", 1)
        sent = dot(resid, w_out_theirs).astype(BF16)
        part = dot(resid, w_out_mine) + swap(sent, "row", 1).astype(F32)
        attn = chip_sum(part).astype(BF16)
        attn = in_order(core, attn, swap(attn, "row", 1), 1)
        return resid, resid_other, attn

    sums_a = forward(own_a)
    sums_other = forward((ffn_other, grad_other))
    back_a, whole_a = backward(sums_a)
    sums_b = forward(own_b)
    back_other, whole_other = backward(sums_other)
    received = swap(back_other.astype(BF16), "seq", 1)
    resid0, resid_other0, attn0 = finish(back_a, received[:step], own_a[1])
    back_b, whole_b = backward(sums_b)
    resid1, resid_other1, attn1 = finish(back_b, received[step:], own_b[1])

    gate_grad, up_grad, hidden = (
        jnp.concatenate(v, 0) for v in zip(whole_a, whole_b, whole_other)
    )
    ffn_all = jnp.concatenate([ffn_input, ffn_other], 0)
    grad_all = jnp.concatenate([out_grad, grad_other], 0)
    gate_wgrad = contract_rows(ffn_all, gate_grad) * norm_factor
    up_wgrad = contract_rows(ffn_all, up_grad) * norm_factor
    down_wgrad = contract_rows(grad_all, hidden) * norm_factor

    resid_grad = jnp.concatenate([resid0, resid1], 0)
    attn_grad = jnp.concatenate([attn0, attn1], 0)
    resid_all = jnp.concatenate([resid_grad, resid_other0, resid_other1], 0)
    mix_all = jnp.concatenate([mix_kept, mix_other], 0)
    out_wgrad = contract_rows(resid_all, mix_all) * norm_factor
    return (resid_grad, attn_grad, gate_wgrad, up_wgrad, down_wgrad, out_wgrad)


def solution(mesh):
    return jax.shard_map(
        per_device,
        mesh=mesh,
        in_specs=(
            P("seq", "row"),
            P("seq", "col"),
            P("seq", "row"),
            P("row", "col"),
            P("row", "col"),
            P("row", "col"),
            P("row", "col"),
        ),
        out_specs=(
            P("seq", "row"),
            P("seq", "col"),
            P("row", ("col", "seq")),
            P("row", ("col", "seq")),
            P("row", ("col", "seq")),
            P("row", ("col", "seq")),
        ),
        check_vma=False,
    )
```

```python
import jax
import jax.numpy as jnp
from jax import lax
from jax.sharding import PartitionSpec as P

BF16 = jnp.bfloat16
F32 = jnp.float32


def swiglu_grads(gate_pre, up_pre, hidden_grad):
    sigmoid_gate = jax.nn.sigmoid(gate_pre)
    activated = gate_pre * sigmoid_gate
    hidden = (activated * up_pre).astype(BF16)
    up_grad = (hidden_grad * activated).astype(BF16)
    slope = sigmoid_gate * (1.0 + gate_pre * (1.0 - sigmoid_gate))
    gate_grad = (hidden_grad * up_pre * slope).astype(BF16)
    return (gate_grad, up_grad, hidden)


def dot(first, second):
    return jnp.dot(first, second, preferred_element_type=F32)


def contract_rows(first, second):
    return lax.dot_general(
        first, second, (((0,), (0,)), ((), ())), preferred_element_type=F32
    )


def contract_cols(first, second):
    return lax.dot_general(
        first, second, (((1,), (1,)), ((), ())), preferred_element_type=F32
    )


def swap(value, axis, bit):
    size = lax.axis_size(axis)
    return lax.ppermute(value, axis, [(i, i ^ bit) for i in range(size)])


def after(value, earlier):
    return lax.optimization_barrier((value, earlier))[0]


def chip_sum(part):
    size = lax.axis_size("row")
    bit = 2
    while bit < size:
        mine = part.astype(BF16)
        part = mine.astype(F32) + swap(mine, "row", bit).astype(F32)
        bit *= 2
    return part


def chip_sum_wide(part):
    size = lax.axis_size("row")
    bit = 2
    received = part
    while bit < size:
        received = swap(part.astype(BF16), "row", bit)
        part = part + received.astype(F32)
        bit *= 2
    return part, received


def in_order(core, mine, theirs, axis):
    return jnp.where(
        core == 0,
        jnp.concatenate([mine, theirs], axis),
        jnp.concatenate([theirs, mine], axis),
    )


def col_scatter(part, gate=None):
    first = None
    if gate is not None:
        part = after(part, gate)
    place = lax.axis_index("col")
    bit = 1
    while bit < lax.axis_size("col"):
        half = part.shape[0] // 2
        high = (place // bit) % 2
        sent = lax.dynamic_slice_in_dim(part, (1 - high) * half, half, 0)
        kept = lax.dynamic_slice_in_dim(part, high * half, half, 0)
        received = swap(sent.astype(BF16), "col", bit)
        first = received if first is None else first
        part = kept + received.astype(F32)
        bit *= 2
    return part, first


def col_share(value):
    place = lax.axis_index("col")
    bit = 1
    while bit < lax.axis_size("col"):
        half = value.shape[0] // 2
        high = (place // bit) % 2
        value = lax.dynamic_slice_in_dim(value, high * half, half, 0)
        bit *= 2
    return value


def col_gather(value, gate):
    place = lax.axis_index("col")
    bit = lax.axis_size("col") // 2
    while bit >= 1:
        high = (place // bit) % 2
        if bit == 1:
            value = after(value, gate)
        value = in_order(high, value, swap(value, "col", bit), 0)
        bit //= 2
    return value


def per_device(ffn_input, attn_mix, out_grad, w_gate, w_up, w_down, w_out):
    core = lax.axis_index("row") % 2
    seq = lax.axis_index("seq")
    tokens, width = ffn_input.shape
    hidden_half = w_gate.shape[1] // 2
    quarter = hidden_half // 2
    head_half = attn_mix.shape[1] // 2
    step = tokens // 2
    norm_factor = (tokens * lax.axis_size("seq")) ** (-0.5)

    own_a = (ffn_input[:step], out_grad[:step])
    own_b = (ffn_input[step:], out_grad[step:])
    ffn_other = swap(ffn_input, "seq", 1)
    grad_other = swap(after(out_grad, ffn_other), "seq", 1)
    mix_sent = lax.dynamic_slice_in_dim(attn_mix, (1 - seq) * head_half, head_half, 1)
    mix_kept = lax.dynamic_slice_in_dim(attn_mix, seq * head_half, head_half, 1)
    mix_other = swap(after(mix_sent, grad_other), "seq", 1)

    def columns(weight, which):
        start = seq * hidden_half + which * quarter
        return lax.dynamic_slice_in_dim(weight, start, quarter, 1)

    mine = [columns(w, core) for w in (w_gate, w_up, w_down)]
    theirs = [columns(w, 1 - core) for w in (w_gate, w_up, w_down)]

    parts, arrived = [], []

    def forward(chunk):
        f, g = chunk
        sums = []
        for x, w_mine, w_theirs in zip((f, f, g), mine, theirs):
            if parts:
                x = after(x, parts[-1])
            if len(arrived) >= 3:
                x = after(x, arrived[-3])
            sent = dot(x, w_theirs).astype(BF16)
            parts.append(dot(x, w_mine) + swap(sent, "row", 1).astype(F32))
            total, received = chip_sum_wide(parts[-1])
            sums.append(total)
            arrived.append(received)
        return sums

    def backward(sums):
        own = swiglu_grads(*sums)
        sibling = [swap(v, "row", 1) for v in own]
        back = (
            contract_cols(own[0], mine[0])
            + contract_cols(own[1], mine[1])
            + contract_cols(sibling[0], theirs[0])
            + contract_cols(sibling[1], theirs[1])
        )
        whole = [in_order(core, a, b, 1) for a, b in zip(own, sibling)]
        return back, whole

    w_out_mine = lax.dynamic_slice_in_dim(w_out, core * head_half, head_half, 1)
    w_out_theirs = lax.dynamic_slice_in_dim(w_out, (1 - core) * head_half, head_half, 1)

    def shares(back, received, grad_chunk, gate=None):
        total, first = col_scatter(back + received.astype(F32), gate)
        return (col_share(grad_chunk).astype(F32) + total).astype(BF16), first

    def attention(resid):
        sent = dot(resid, w_out_theirs).astype(BF16)
        part = dot(resid, w_out_mine) + swap(sent, "row", 1).astype(F32)
        attn = chip_sum(part).astype(BF16)
        return in_order(core, attn, swap(attn, "row", 1), 1)

    sums_a = forward(own_a)
    sums_other = forward((ffn_other, grad_other))
    back_a, whole_a = backward(sums_a)
    sums_b = forward(own_b)
    back_other, whole_other = backward(sums_other)
    back_sent = after(back_other.astype(BF16), mix_other)
    received = swap(back_sent, "seq", 1)
    back_b, whole_b = backward([after(v, back_sent) for v in sums_b])
    share0, first = shares(back_a, received[:step], own_a[1])

    gate_grad, up_grad, hidden = (
        jnp.concatenate(v, 0) for v in zip(whole_a, whole_b, whole_other)
    )
    ffn_all = jnp.concatenate([ffn_input, ffn_other], 0)
    grad_all = jnp.concatenate([out_grad, grad_other], 0)
    gate_wgrad = contract_rows(ffn_all, gate_grad) * norm_factor
    share1, _ = shares(back_b, received[step:], own_b[1], (first, gate_wgrad))
    up_wgrad = contract_rows(ffn_all, after(up_grad, first)) * norm_factor
    down_wgrad = contract_rows(grad_all, after(hidden, share0)) * norm_factor

    resid0 = col_gather(share0, first)
    resid1 = col_gather(after(share1, up_wgrad), down_wgrad)
    resid_other0 = swap(resid0, "seq", 1)
    resid_other1 = swap(resid1, "seq", 1)
    attn0, attn1 = attention(resid0), attention(resid1)
    resid_grad = jnp.concatenate([resid0, resid1], 0)
    attn_grad = jnp.concatenate([attn0, attn1], 0)
    resid_all = jnp.concatenate([resid_grad, resid_other0, resid_other1], 0)
    mix_all = jnp.concatenate([mix_kept, mix_other], 0)
    out_wgrad = contract_rows(resid_all, mix_all) * norm_factor
    return (resid_grad, attn_grad, gate_wgrad, up_wgrad, down_wgrad, out_wgrad)


def solution(mesh):
    return jax.shard_map(
        per_device,
        mesh=mesh,
        in_specs=(
            P("seq", "row"),
            P("seq", "col"),
            P("seq", "row"),
            P("row", "col"),
            P("row", "col"),
            P("row", "col"),
            P("row", "col"),
        ),
        out_specs=(
            P("seq", "row"),
            P("seq", "col"),
            P("row", ("col", "seq")),
            P("row", ("col", "seq")),
            P("row", ("col", "seq")),
            P("row", ("col", "seq")),
        ),
        check_vma=False,
    )
```
